32 devices in a mesh: lon: 8 (over z, core), lat: 2 (over y), tp: 2 (over x).
Axes of the slice: x: 2, y: 2, z: 4, core: 2. Of those that a mesh axis runs over, the one named last changes fastest.
Arguments:
- latent: bfloat16 [96, 24, 4, 512], P('lon', 'lat'), may hold values from -6 to 6
- cotangent: bfloat16 [96, 24, 4, 512], P('lon', 'lat'), may hold values from -6 to 6
- ln_gain: float32 [512], replicated, may hold values from 0.1 to 1.9
- w_qkv: bfloat16 [3, 512, 512], P(None, None, 'tp'), may hold values from -0.25 to 0.25
- w_out: bfloat16 [512, 512], P('tp'), may hold values from -0.25 to 0.25
- bias_table: float32 [4, 2, 8, 3312], P('lat', None, 'tp'), may hold values from -3 to 360
Outputs:
- output: bfloat16 [96, 24, 4, 512], P('lon', 'lat')
- grad_latent: bfloat16 [96, 24, 4, 512], P('lon', 'lat')
- grad_gain: float32 [512], replicated
- grad_wqkv: float32 [3, 512, 512], P(None, None, 'tp')
- grad_wout: float32 [512, 512], P('tp')
- grad_bias: float32 [4, 2, 8, 3312], P('lat', None, 'tp')
The draws below stay inside these ranges and needn't reach their ends.
All inputs are finite; a program needn't handle non-finite values.
Results may differ from the reference program's by a relative error of at most 0.023.
Values may be sent and summed in bfloat16 or wider, within the bound.
A program may use at most 128 MiB of HBM per device.

```python
import math
import jax
import jax.numpy as jnp
import numpy as np
from jax import lax

D = 512
HEADS = 8
HD = 64
WLON = 12
WLAT = 6
WLEV = 2
LEV = 4
NLON = 96
NLAT = 24
WTOK = 144
NREL = 3312
LATWIN = 4
LEVWIN = 2
N_TP = 2


def draw_bias_table(key, part):
    key = jax.random.fold_in(key, 7)
    shape = (LATWIN, LEVWIN, HEADS, WLEV * WLEV, WLAT * WLAT, 2 * WLON - 1)
    base = jnp.clip(0.5 * jax.random.normal(key, shape, jnp.float32), -3.0, 3.0)
    return base.reshape(LATWIN, LEVWIN, HEADS, NREL).astype(jnp.float32)


def block_scale(own_key, shape, shards, low, high):
    gain = 1.0
    for dim, parts in shards:
        steps = jax.random.uniform(jax.random.fold_in(jax.random.fold_in(own_key, 6), dim), (parts,), jnp.float32, low / len(shards), high / len(shards))
        gain = gain * jnp.repeat(jnp.exp(steps), shape[dim] // parts).reshape((-1,) + (1,) * (len(shape) - 1 - dim))
    return gain


def bell_draw(rng, extent, width, most, shards=(), dtype=jnp.bfloat16):
    drawn = jax.random.normal(rng, extent, jnp.float32) * width
    if len(shards) > 0:
        drawn = block_scale(rng, extent, shards, -0.22, 0.18) * drawn
    return jnp.clip(drawn, min=-most, max=most).astype(dtype)


def setup_inputs(seed: int = 0) -> dict:
    arg_keys = jax.random.split(jax.random.key(seed), 7)
    return {
        "latent": bell_draw(arg_keys[0], (NLON, NLAT, LEV, D), 1.0, 6.0, ((0, 8), (1, 2))),
        "cotangent": bell_draw(arg_keys[1], (NLON, NLAT, LEV, D), 1.0, 6.0, ((0, 8), (1, 2))),
        "ln_gain": jnp.clip(1.0 + 0.18 * jax.random.normal(arg_keys[2], (D,), jnp.float32), 0.1, 1.9),
        "w_qkv": bell_draw(arg_keys[3], (3, D, D), D ** -0.5, 0.25, ((2, 2),)),
        "w_out": bell_draw(arg_keys[4], (D, D), D ** -0.5, 0.25, ((0, 2),)),
        "bias_table": draw_bias_table(jax.random.fold_in(arg_keys[6], 71), 0),
    }


def pair_layout():
    position = np.arange(WTOK)
    lon_pos = position // (WLAT * WLEV)
    lat_pos = position // WLEV % WLAT
    lev_pos = position % WLEV
    relative = lon_pos[None, :] - lon_pos[:, None] + WLON - 1
    entries = ((lev_pos[:, None] * WLEV + lev_pos[None, :]) * WLAT * WLAT + lat_pos[:, None] * WLAT + lat_pos[None, :]) * (2 * WLON - 1) + relative
    return (entries.astype(np.int32), lat_pos, lev_pos)

def to_windows(values):
    lon_cells, lat_cells, lev_cells, channels = values.shape
    blocks = values.reshape(lon_cells // WLON, WLON, lat_cells // WLAT, WLAT, lev_cells // WLEV, WLEV, channels)
    blocks = blocks.transpose(2, 4, 0, 1, 3, 5, 6)
    return blocks.reshape(lat_cells // WLAT, lev_cells // WLEV, lon_cells // WLON, WTOK, channels)

def from_windows(values):
    lat_bands, lev_bands, lon_bands, window_len, channels = values.shape
    blocks = values.reshape(lat_bands, lev_bands, lon_bands, WLON, WLAT, WLEV, channels)
    blocks = blocks.transpose(2, 3, 0, 4, 1, 5, 6)
    return blocks.reshape(lon_bands * WLON, lat_bands * WLAT, lev_bands * WLEV, channels)

def allowed_pairs(last_lat, lev_bands, lat_pos, lev_pos):
    lat_edge = jnp.asarray(lat_pos >= WLAT - WLAT // 2)
    lev_edge = jnp.asarray(lev_pos >= WLEV - WLEV // 2)
    lev_last = jnp.arange(lev_bands) == lev_bands - 1
    lat_region = last_lat[:, None] & lat_edge[None, :]
    lev_region = lev_last[:, None] & lev_edge[None, :]
    same_lat = lat_region[:, :, None] == lat_region[:, None, :]
    same_lev = lev_region[:, :, None] == lev_region[:, None, :]
    return same_lat[:, None] & same_lev[None, :]

def layer_norm(values, scale_gain):
    values = values.astype(jnp.float32)
    centre = lax.optimization_barrier(jnp.mean(values, -1, keepdims=True))
    shifted = values - centre
    inv_std = lax.rsqrt(lax.optimization_barrier(jnp.mean(shifted * shifted, -1, keepdims=True)) + 1e-05)
    normed = shifted * inv_std
    return (normed, inv_std, (normed * scale_gain).astype(jnp.bfloat16))

def rounded_sum(partials):
    total = jnp.zeros(partials[0].shape, jnp.float32)
    for partial_value in partials:
        total = total + lax.optimization_barrier(partial_value.astype(jnp.bfloat16)).astype(jnp.float32)
    return total.astype(jnp.bfloat16)

def reference(latent, cotangent, ln_gain, w_qkv, w_out, bias_table):
    entries, lat_pos, lev_pos = pair_layout()
    entry_ids = jnp.asarray(entries)
    shifts = (-(WLON // 2), -(WLAT // 2), -(WLEV // 2))
    scale_gain = ln_gain.astype(jnp.float32)
    inv_scale = 1.0 / math.sqrt(HD)
    group_width = D // N_TP

    def bands_of(values):
        rolled = jnp.roll(values, shifts, axis=(0, 1, 2))
        return rolled.reshape(NLON, LATWIN, WLAT, LEV, D).transpose(1, 0, 2, 3, 4)

    def band_step(carry, band):
        grad_qkv, grad_out, grad_gain = carry
        latent_band, cot_band, table_band, band_number = band
        latent_win = to_windows(latent_band)
        cot_win = to_windows(cot_band)
        lev_bands = latent_win.shape[1]
        lon_bands = latent_win.shape[2]
        last_lat = jnp.reshape(band_number == LATWIN - 1, (1,))
        allowed = allowed_pairs(last_lat, lev_bands, lat_pos, lev_pos)
        bias_full = jnp.take(table_band, entry_ids, axis=2)[None]
        normed, inv_std, hidden = layer_norm(latent_win, scale_gain)
        hidden_flat = hidden.reshape(-1, D)
        head_shape = (1, lev_bands, lon_bands, WTOK, HEADS, HD)
        projected = [jnp.dot(hidden_flat, w_qkv[member], preferred_element_type=jnp.float32).astype(jnp.bfloat16) for member in range(3)]
        queries, key_rows, value_rows = [matrix.reshape(head_shape).astype(jnp.float32) for matrix in projected]
        scores = jnp.einsum('abwqhe,abwkhe->abwhqk', queries, key_rows) * inv_scale + bias_full[:, :, None]
        scores = jnp.where(allowed[:, :, None, None], scores, -jnp.inf)
        row_max = lax.optimization_barrier(jnp.max(scores, -1, keepdims=True))
        expsum = jnp.exp(scores - row_max)
        attn_weights = expsum / lax.optimization_barrier(jnp.sum(expsum, -1, keepdims=True))
        attn_low = attn_weights.astype(jnp.bfloat16)
        attended = jnp.einsum('abwhqk,abwkhe->abwqhe', attn_low.astype(jnp.float32), value_rows).astype(jnp.bfloat16)
        attended_flat = attended.reshape(-1, D)
        out_terms = [jnp.dot(attended_flat[:, group * group_width:(group + 1) * group_width], w_out[group * group_width:(group + 1) * group_width], preferred_element_type=jnp.float32) for group in range(N_TP)]
        attn_out = rounded_sum(out_terms)
        result = (latent_win.reshape(-1, D).astype(jnp.float32) + attn_out.astype(jnp.float32)).astype(jnp.bfloat16)
        cot_flat = cot_win.reshape(-1, D)
        grad_out = grad_out + jnp.dot(attended_flat.T, cot_flat, preferred_element_type=jnp.float32)
        down_heads = jnp.dot(cot_flat, w_out.T, preferred_element_type=jnp.float32).astype(jnp.bfloat16).reshape(head_shape).astype(jnp.float32)
        down_scores = jnp.einsum('abwqhe,abwkhe->abwhqk', down_heads, value_rows)
        grad_values = jnp.einsum('abwhqk,abwqhe->abwkhe', attn_low.astype(jnp.float32), down_heads).astype(jnp.bfloat16)
        centred = lax.optimization_barrier(jnp.sum(down_scores * attn_weights, -1, keepdims=True))
        grad_scores = attn_weights * (down_scores - centred)
        bias_terms = lax.optimization_barrier(jnp.sum(grad_scores, 2))
        grad_table = jax.ops.segment_sum(bias_terms.reshape(-1, WTOK * WTOK).T, entry_ids.reshape(-1), num_segments=NREL).T
        grad_table = grad_table.reshape(table_band.shape)
        scores_low = grad_scores.astype(jnp.bfloat16).astype(jnp.float32)
        grad_queries = (jnp.einsum('abwhqk,abwkhe->abwqhe', scores_low, key_rows) * inv_scale).astype(jnp.bfloat16)
        grad_keys = (jnp.einsum('abwhqk,abwqhe->abwkhe', scores_low, queries) * inv_scale).astype(jnp.bfloat16)
        grads_proj = [matrix.reshape(-1, D) for matrix in (grad_queries, grad_keys, grad_values)]
        grad_qkv = grad_qkv + jnp.stack([jnp.dot(hidden_flat.T, matrix, preferred_element_type=jnp.float32) for matrix in grads_proj])
        hidden_terms = []
        for group in range(N_TP):
            columns = slice(group * group_width, (group + 1) * group_width)
            partial_value = jnp.zeros((hidden_flat.shape[0], D), jnp.float32)
            for member in range(3):
                partial_value = partial_value + jnp.dot(grads_proj[member][:, columns], w_qkv[member][:, columns].T, preferred_element_type=jnp.float32)
            hidden_terms.append(partial_value)
        grad_hidden = rounded_sum(hidden_terms).astype(jnp.float32)
        normed_flat = normed.reshape(-1, D)
        inv_flat = inv_std.reshape(-1, 1)
        scaled = grad_hidden * scale_gain
        grad_in = cot_flat.astype(jnp.float32) + inv_flat * (scaled - lax.optimization_barrier(jnp.mean(scaled, -1, keepdims=True)) - normed_flat * lax.optimization_barrier(jnp.mean(scaled * normed_flat, -1, keepdims=True)))
        grad_gain = grad_gain + lax.optimization_barrier(jnp.sum(grad_hidden * normed_flat, 0))
        win_shape = latent_win.shape
        result_band = from_windows(result.reshape(win_shape))
        grad_band = from_windows(grad_in.astype(jnp.bfloat16).reshape(win_shape))
        return ((grad_qkv, grad_out, grad_gain), (result_band, grad_band, grad_table))
    init = (jnp.zeros((3, D, D), jnp.float32), jnp.zeros((D, D), jnp.float32), jnp.zeros((D,), jnp.float32))
    band_ids = jnp.arange(LATWIN).astype(jnp.int32)
    carry, stacked = lax.scan(band_step, init, (bands_of(latent), bands_of(cotangent), bias_table, band_ids))
    grad_wqkv, grad_wout, grad_gain = carry
    result_bands, grad_bands, grad_bias = stacked

    def unbands(values):
        whole = values.transpose(1, 0, 2, 3, 4).reshape(NLON, NLAT, LEV, D)
        return jnp.roll(whole, (WLON // 2, WLAT // 2, WLEV // 2), axis=(0, 1, 2))
    return (unbands(result_bands), unbands(grad_bands), grad_gain, grad_wqkv, grad_wout, grad_bias)
```

```python
import math

import jax
import jax.numpy as jnp
import numpy as np
from jax import lax
from jax.experimental import pallas as pl
from jax.experimental.pallas import tpu as pltpu
from jax.sharding import PartitionSpec as P

HD = 64
WLON = 12
WLAT = 6
WLEV = 2
WTOK = 144
NREL = 3312
NDIFF = 2 * WLON - 1
CELL = WLAT * WLEV
WIDE = NDIFF * CELL
F32 = jnp.float32
BF16 = jnp.bfloat16


def spread_matrices():
    spread = np.zeros((WLEV, WLAT * NDIFF, WIDE), np.float32)
    for lev in range(WLEV):
        for row in range(WLAT):
            for diff in range(NDIFF):
                spread[lev, row * NDIFF + diff, diff * CELL + lev * WLAT + row] = 1.0
    return spread


def shift_along(shard, lon_by, lat_by):
    lon_count = lax.axis_size("lon")
    lat_count = lax.axis_size("lat")
    pairs = []
    for i in range(lon_count):
        for j in range(lat_count):
            target = ((i + lon_by) % lon_count) * lat_count + (j + lat_by) % lat_count
            pairs.append((i * lat_count + j, target))
    return lax.ppermute(shard, ("lon", "lat"), pairs)


def enter(values):
    lon_half = WLON // 2
    lat_half = WLAT // 2
    corner = shift_along(values[:lon_half, :lat_half], -1, -1)
    lon_part = shift_along(values[:lon_half, lat_half:], -1, 0)
    lat_part = shift_along(values[lon_half:, :lat_half], 0, -1)
    near = jnp.concatenate([values[lon_half:, lat_half:], lat_part], 1)
    far = jnp.concatenate([lon_part, corner], 1)
    values = jnp.concatenate([near, far], 0)
    return jnp.roll(values, -(WLEV // 2), axis=2)


def leave(values):
    lon_half = WLON // 2
    lat_half = WLAT // 2
    values = jnp.roll(values, WLEV // 2, axis=2)
    lon_cut = values.shape[0] - lon_half
    lat_cut = values.shape[1] - lat_half
    corner = shift_along(values[lon_cut:, lat_cut:], 1, 1)
    lon_part = shift_along(values[lon_cut:, :lat_cut], 1, 0)
    lat_part = shift_along(values[:lon_cut, lat_cut:], 0, 1)
    near = jnp.concatenate([corner, lon_part], 1)
    far = jnp.concatenate([lat_part, values[:lon_cut, :lat_cut]], 1)
    return jnp.concatenate([near, far], 0)


def to_windows(values):
    lon_cells, lat_cells, lev_cells, channels = values.shape
    blocks = values.reshape(
        lon_cells // WLON, WLON, lat_cells // WLAT, WLAT, lev_cells // WLEV, WLEV, channels
    )
    blocks = blocks.transpose(2, 4, 0, 1, 5, 3, 6)
    return blocks.reshape(-1, WTOK, channels)


def from_windows(values, lat_bands, lev_bands, lon_bands):
    channels = values.shape[-1]
    blocks = values.reshape(lat_bands, lev_bands, lon_bands, WLON, WLEV, WLAT, channels)
    blocks = blocks.transpose(2, 3, 0, 5, 1, 4, 6)
    return blocks.reshape(lon_bands * WLON, lat_bands * WLAT, lev_bands * WLEV, channels)


def mm(a, b):
    return lax.dot_general(a, b, (((1,), (0,)), ((), ())), preferred_element_type=F32)


def mm_nt(a, b):
    return lax.dot_general(a, b, (((1,), (1,)), ((), ())), preferred_element_type=F32)


def mm_tn(a, b):
    return lax.dot_general(a, b, (((0,), (0,)), ((), ())), preferred_element_type=F32)


def core_kernel(
    head_count,
    lat_ref,
    cot_ref,
    gain_ref,
    wqkv_ref,
    wout_ref,
    table_ref,
    col_ref,
    row_ref,
    out_ref,
    gh_ref,
    gqkv_ref,
    gout_ref,
    gtab_ref,
    hidden_s,
    grads_s,
    att_s,
    cot_s,
    bias_s,
    gtab_s,
):
    step = pl.program_id(0)
    rows = pl.ds(pl.multiple_of(step * WTOK, 16), WTOK)
    inv_scale = 1.0 / math.sqrt(HD)
    width = head_count * HD
    x = lat_ref[0].astype(F32)
    shifted = x - jnp.mean(x, -1, keepdims=True)
    inv_std = lax.rsqrt(jnp.mean(shifted * shifted, -1, keepdims=True) + 1e-05)
    hidden = (shifted * inv_std * gain_ref[...]).astype(BF16)
    hidden_s[rows] = hidden
    cot = cot_ref[0]
    cot_s[rows] = cot
    queries = mm(hidden, wqkv_ref[0]).astype(BF16)
    keys = mm(hidden, wqkv_ref[1]).astype(BF16)
    vals = mm(hidden, wqkv_ref[2]).astype(BF16)
    down = mm_nt(cot, wout_ref[...]).astype(BF16)
    allowed = col_ref[0] == row_ref[0]
    att_parts, gq_parts, gk_parts, gv_parts = [], [], [], []
    for head in range(head_count):
        cols = slice(head * HD, (head + 1) * HD)
        q, k, v, d = queries[:, cols], keys[:, cols], vals[:, cols], down[:, cols]
        table = table_ref[0, head]
        for lon_pos in range(WLON):
            start = (WLON - 1 - lon_pos) * CELL
            bias_s[head, lon_pos * CELL : (lon_pos + 1) * CELL, :] = table[:, start : start + WTOK]
        scores = mm_nt(q, k) * inv_scale + bias_s[head]
        scores = jnp.where(allowed, scores, -jnp.inf)
        expsum = jnp.exp(scores - jnp.max(scores, -1, keepdims=True))
        probs = expsum / jnp.sum(expsum, -1, keepdims=True)
        low = probs.astype(BF16)
        att_parts.append(mm(low, v).astype(BF16))
        dp = mm_nt(d, v)
        gv_parts.append(mm_tn(low, d).astype(BF16))
        ds = probs * (dp - jnp.sum(dp * probs, -1, keepdims=True))
        bias_s[head] = ds
        gtab_s[head] = jnp.zeros((CELL, WIDE), F32)
        for lon_pos in range(WLON):
            start = (WLON - 1 - lon_pos) * CELL
            gtab_s[head, :, start : start + WTOK] += bias_s[
                head, lon_pos * CELL : (lon_pos + 1) * CELL, :
            ]
        gtab_ref[0, head] = gtab_s[head].astype(BF16)
        ds_low = ds.astype(BF16)
        gq_parts.append((mm(ds_low, k) * inv_scale).astype(BF16))
        gk_parts.append((mm_tn(ds_low, q) * inv_scale).astype(BF16))
    att = jnp.concatenate(att_parts, 1)
    att_s[rows] = att
    gq = jnp.concatenate(gq_parts, 1)
    gk = jnp.concatenate(gk_parts, 1)
    gv = jnp.concatenate(gv_parts, 1)
    grads_s[0, rows] = gq
    grads_s[1, rows] = gk
    grads_s[2, rows] = gv
    out_ref[0] = mm(att, wout_ref[...]).astype(BF16)
    gh = mm_nt(gq, wqkv_ref[0])
    gh = gh + mm_nt(gk, wqkv_ref[1])
    gh = gh + mm_nt(gv, wqkv_ref[2])
    gh_ref[0] = gh.astype(BF16)

    @pl.when(step == pl.num_programs(0) - 1)
    def _():
        for member in range(3):
            gqkv_ref[member] = mm_tn(hidden_s[...], grads_s[member]).astype(BF16)
        gout_ref[...] = mm_tn(att_s[...], cot_s[...]).astype(BF16)


def core(lat_win, cot_win, ln_gain, w_qkv, w_out, table, region):
    windows, _, model_width = lat_win.shape
    local_width = w_out.shape[0]
    head_count = local_width // HD
    tokens = windows * WTOK
    whole = lambda *shape: pl.BlockSpec(shape, lambda i: (0,) * len(shape))
    each = lambda *shape: pl.BlockSpec((1,) + shape, lambda i: (i,) + (0,) * len(shape))
    return pl.pallas_call(
        lambda *refs: core_kernel(head_count, *refs),
        grid=(windows,),
        in_specs=[
            each(WTOK, model_width),
            each(WTOK, model_width),
            whole(1, model_width),
            whole(3, model_width, local_width),
            whole(local_width, model_width),
            each(head_count, CELL, WIDE),
            each(WTOK, 1),
            each(1, WTOK),
        ],
        out_specs=[
            each(WTOK, model_width),
            each(WTOK, model_width),
            whole(3, model_width, local_width),
            whole(local_width, model_width),
            each(head_count, CELL, WIDE),
        ],
        out_shape=[
            jax.ShapeDtypeStruct((windows, WTOK, model_width), BF16),
            jax.ShapeDtypeStruct((windows, WTOK, model_width), BF16),
            jax.ShapeDtypeStruct((3, model_width, local_width), BF16),
            jax.ShapeDtypeStruct((local_width, model_width), BF16),
            jax.ShapeDtypeStruct((windows, head_count, CELL, WIDE), BF16),
        ],
        scratch_shapes=[
            pltpu.VMEM((tokens, model_width), BF16),
            pltpu.VMEM((3, tokens, local_width), BF16),
            pltpu.VMEM((tokens, local_width), BF16),
            pltpu.VMEM((tokens, model_width), BF16),
            pltpu.VMEM((head_count, WTOK, WTOK), F32),
            pltpu.VMEM((head_count, CELL, WIDE), F32),
        ],
        compiler_params=pltpu.CompilerParams(vmem_limit_bytes=40 * 1024 * 1024),
        cost_estimate=pl.CostEstimate(
            flops=4 * 10**9, bytes_accessed=8 * 10**6, transcendentals=331776
        ),
    )(lat_win, cot_win, ln_gain.reshape(1, -1), w_qkv, w_out, table, region[:, :, None], region[:, None, :])


def on_device(latent, cotangent, ln_gain, w_qkv, w_out, bias_table):
    lon_cells, lat_cells, lev_cells, model_width = latent.shape
    head_count = w_out.shape[0] // HD
    lat_bands = lat_cells // WLAT
    lev_bands = lev_cells // WLEV
    lon_bands = lon_cells // WLON
    windows = lat_bands * lev_bands * lon_bands
    spread = spread_matrices()

    joined = jnp.concatenate([latent, cotangent], 3)
    rolled = enter(joined)
    lat_win = to_windows(rolled[..., :model_width])
    cot_win = to_windows(rolled[..., model_width:])

    last_device = lax.axis_index("lat") == lax.axis_size("lat") - 1
    position = np.arange(WTOK)
    lat_edge = position % WLAT >= WLAT - WLAT // 2
    lev_edge = position // WLAT % WLEV >= WLEV - WLEV // 2
    lat_last = last_device & (jnp.arange(lat_bands) == lat_bands - 1)
    lev_last = jnp.arange(lev_bands) == lev_bands - 1
    region = (
        2.0 * (lat_last[:, None] & lat_edge).astype(F32)[:, None]
        + (lev_last[:, None] & lev_edge).astype(F32)[None]
    )
    region = jnp.broadcast_to(region[:, :, None], (lat_bands, lev_bands, lon_bands, WTOK))
    region = region.reshape(windows, WTOK)

    grouped = bias_table.reshape(
        lat_bands, lev_bands, head_count, WLEV, WLEV, WLAT, WLAT * NDIFF
    )
    table = sum(
        jnp.einsum(
            "abhtrd,dw->abhtrw", grouped[:, :, :, :, lev], spread[lev], precision=lax.Precision.HIGHEST
        )
        for lev in range(WLEV)
    )
    table = table.reshape(lat_bands * lev_bands, head_count, CELL, WIDE)
    if lon_bands > 1:
        table = jnp.repeat(table, lon_bands, axis=0)

    out_win, gh_win, grad_qkv_local, grad_out_local, grad_tab = core(
        lat_win, cot_win, ln_gain, w_qkv, w_out, table, region
    )
    if lon_bands > 1:
        grad_tab = jnp.sum(
            grad_tab.reshape(lat_bands * lev_bands, lon_bands, head_count, CELL, WIDE).astype(F32), 1
        ).astype(BF16)

    both = lax.psum(jnp.concatenate([out_win, gh_win], -1), "tp")
    both = leave(from_windows(both, lat_bands, lev_bands, lon_bands))
    out_own = both[..., :model_width]
    grad_own = both[..., model_width:]
    output = (latent.astype(F32) + out_own.astype(F32)).astype(BF16)

    values = latent.astype(F32)
    shifted = values - jnp.mean(values, -1, keepdims=True)
    inv_std = lax.rsqrt(jnp.mean(shifted * shifted, -1, keepdims=True) + 1e-05)
    normed = shifted * inv_std
    grad_float = grad_own.astype(F32)
    scaled = grad_float * ln_gain
    grad_latent = (
        cotangent.astype(F32)
        + inv_std
        * (
            scaled
            - jnp.mean(scaled, -1, keepdims=True)
            - normed * jnp.mean(scaled * normed, -1, keepdims=True)
        )
    ).astype(BF16)
    gain_local = jnp.sum((grad_float * normed).reshape(-1, model_width), 0)
    grad_wqkv, grad_wout = lax.psum((grad_qkv_local, grad_out_local), ("lon", "lat"))
    grad_gain = lax.psum(gain_local, ("lon", "lat"))
    grad_tab = lax.psum(grad_tab, "lon")
    grad_tab = grad_tab.reshape(lat_bands, lev_bands, head_count, WLEV, WLAT, WIDE)
    grad_bias = jnp.stack(
        [
            jnp.einsum(
                "abhtrw,dw->abhtrd", grad_tab, spread[lev].astype(BF16), preferred_element_type=F32
            )
            for lev in range(WLEV)
        ],
        axis=4,
    ).reshape(bias_table.shape)
    return (
        output,
        grad_latent,
        grad_gain,
        grad_wqkv.astype(F32),
        grad_wout.astype(F32),
        grad_bias,
    )


def solution(mesh):
    return jax.shard_map(
        on_device,
        mesh=mesh,
        in_specs=(
            P("lon", "lat", None, None),
            P("lon", "lat", None, None),
            P(),
            P(None, None, "tp"),
            P("tp", None),
            P("lat", None, "tp", None),
        ),
        out_specs=(
            P("lon", "lat", None, None),
            P("lon", "lat", None, None),
            P(),
            P(None, None, "tp"),
            P("tp", None),
            P("lat", None, "tp", None),
        ),
        check_vma=False,
    )
```

```python
import math

import jax
import jax.numpy as jnp
import numpy as np
from jax import lax
from jax.experimental import pallas as pl
from jax.experimental.pallas import tpu as pltpu
from jax.sharding import PartitionSpec as P

HD = 64
WLON = 12
WLAT = 6
WLEV = 2
WTOK = 144
NREL = 3312
NDIFF = 2 * WLON - 1
CELL = WLAT * WLEV
WIDE = NDIFF * CELL
F32 = jnp.float32
BF16 = jnp.bfloat16


def spread_matrices():
    spread = np.zeros((WLEV, WLAT * NDIFF, WIDE), np.float32)
    for lev in range(WLEV):
        for row in range(WLAT):
            for diff in range(NDIFF):
                spread[lev, row * NDIFF + diff, diff * CELL + lev * WLAT + row] = 1.0
    return spread


def mm(a, b):
    return lax.dot_general(a, b, (((1,), (0,)), ((), ())), preferred_element_type=F32)


def mm_nt(a, b):
    return lax.dot_general(a, b, (((1,), (1,)), ((), ())), preferred_element_type=F32)


def mm_tn(a, b):
    return lax.dot_general(a, b, (((0,), (0,)), ((), ())), preferred_element_type=F32)


def round_up(count, to):
    return -(-count // to) * to


def halo_layout(lon_cells, lat_cells, lev_cells):
    lon_half, lat_half, lev_half = WLON // 2, WLAT // 2, WLEV // 2
    tokens = lon_cells * lat_cells * lev_cells
    cells = np.arange(tokens).reshape(lon_cells, lat_cells, lev_cells)
    pieces = [
        cells[:lon_half, lat_half:],
        cells[lon_half:, :lat_half],
        cells[:lon_half, :lat_half],
    ]
    starts, total = [], 0
    for piece in pieces:
        starts.append((total, round_up(piece.size, 16)))
        total += round_up(piece.size, 16)
    gather = np.zeros((total, tokens), np.float32)
    slots = []
    for piece, (start, _) in zip(pieces, starts):
        gather[start + np.arange(piece.size), piece.reshape(-1)] = 1.0
        slots.append(tokens + start + np.arange(piece.size).reshape(piece.shape))
    near = np.concatenate([cells[lon_half:, lat_half:], slots[1]], 1)
    far = np.concatenate([slots[0], slots[2]], 1)
    rolled = np.roll(np.concatenate([near, far], 0), -lev_half, axis=2)
    lonb, latb, levb = lon_cells // WLON, lat_cells // WLAT, lev_cells // WLEV
    order = rolled.reshape(lonb, WLON, latb, WLAT, levb, WLEV)
    order = order.transpose(2, 4, 0, 1, 5, 3).reshape(-1)
    place = np.zeros((tokens, tokens + total), np.float32)
    place[np.arange(tokens), order] = 1.0
    return gather, place[:, :tokens], place[:, tokens:], starts


def fused_kernel(
    cfg,
    x_ref,
    gain_ref,
    wqkv_ref,
    wout_ref,
    table_ref,
    col_ref,
    row_ref,
    gather_ref,
    own_ref,
    arrived_ref,
    gather_t_ref,
    own_t_ref,
    arrived_t_ref,
    out_ref,
    glat_ref,
    gqkv_ref,
    gout_ref,
    gtab_ref,
    ggain_ref,
    pack_s,
    halo_s,
    back_s,
    win_s,
    hidden_s,
    grads_s,
    att_s,
    bias_s,
    gtab_s,
    mine_s,
    theirs_s,
    wg_s,
    wg_core,
    wg_a,
    wg_lat,
    wg_b,
    wg_z,
    wg_zg,
    wg_lg,
    wg_cg,
    tab_s,
    tab_core,
    tab_a,
    tab_z,
    tab_zg,
    tab_cg,
    gain_s,
    in_send,
    in_recv,
    tp_send,
    tp_recv,
    out_send,
    out_recv,
    core_send,
    core_recv,
    lat_send,
    lat_recv,
    z_send,
    z_recv,
    tz_send,
    tz_recv,
    gain_send,
    gain_recv,
):
    heads, windows, starts, n_lon, n_lat, n_tp = cfg
    n_z = n_lon // 2
    model_width = gain_ref.shape[1]
    inv_scale = 1.0 / math.sqrt(HD)
    lon, lat, tp = lax.axis_index("lon"), lax.axis_index("lat"), lax.axis_index("tp")
    z, core = lax.div(lon, 2), lax.rem(lon, 2)
    sibling = lon + 1 - 2 * core
    group = lat * n_tp + tp

    def device(lon_at, lat_at, tp_at):
        return {"lon": lon_at, "lat": lat_at, "tp": tp_at}

    def send(src, dst, send_sem, recv_sem, where):
        return pltpu.make_async_remote_copy(
            src_ref=src,
            dst_ref=dst,
            send_sem=send_sem,
            recv_sem=recv_sem,
            device_id=where,
            device_id_type=pl.DeviceIdType.MESH,
        )

    lon_next, lon_prev = lax.rem(lon + 1, n_lon), lax.rem(lon + n_lon - 1, n_lon)
    lat_next, lat_prev = lax.rem(lat + 1, n_lat), lax.rem(lat + n_lat - 1, n_lat)
    before = [
        device(lon_prev, lat, tp),
        device(lon, lat_prev, tp),
        device(lon_prev, lat_prev, tp),
    ]
    after = [
        device(lon_next, lat, tp),
        device(lon, lat_next, tp),
        device(lon_next, lat_next, tp),
    ]
    z_peers = [device(lax.rem(z + d, n_z) * 2 + core, lat, tp) for d in range(1, n_z)]
    lat_peers = [device(lon, lax.rem(lat + d, n_lat), tp) for d in range(1, n_lat)]
    group_peers = []
    for d in range(1, n_lat * n_tp):
        other = lax.rem(group + d, n_lat * n_tp)
        group_peers.append(device(lon, lax.div(other, n_tp), lax.rem(other, n_tp)))
    core_peer = device(sibling, lat, tp)
    tp_peer = device(lon, lat, lax.rem(tp + 1, n_tp))

    barrier = pltpu.get_barrier_semaphore()
    greeted = before + after + z_peers + group_peers + [core_peer]
    for where in greeted:
        pl.semaphore_signal(
            barrier, inc=1, device_id=where, device_id_type=pl.DeviceIdType.MESH
        )
    pack_s[...] = mm(gather_ref[...], x_ref[...]).astype(BF16)
    pl.semaphore_wait(barrier, len(greeted))
    halo = [
        send(
            pack_s.at[pl.ds(start, size)],
            halo_s.at[pl.ds(start, size)],
            in_send.at[i],
            in_recv.at[i],
            before[i],
        )
        for i, (start, size) in enumerate(starts)
    ]
    for copy in halo:
        copy.start()
    win_s[...] = mm(own_ref[...], x_ref[...]).astype(BF16)
    for copy in halo:
        copy.wait()
    win_s[...] += mm(arrived_ref[...], halo_s[...]).astype(BF16)

    gain_s[group] = jnp.zeros(gain_s.shape[1:], F32)

    def tp_copy(w):
        rows = pl.ds(pl.multiple_of(w * WTOK, 16), WTOK)
        return send(mine_s.at[rows], theirs_s.at[rows], tp_send.at[w], tp_recv.at[w], tp_peer)

    def window(w, carry):
        rows = pl.ds(pl.multiple_of(w * WTOK, 16), WTOK)
        x = win_s[rows, :model_width].astype(F32)
        cot = win_s[rows, model_width:]
        shifted = x - jnp.mean(x, -1, keepdims=True)
        inv_std = lax.rsqrt(jnp.mean(shifted * shifted, -1, keepdims=True) + 1e-05)
        normed = shifted * inv_std
        hidden = (normed * gain_ref[...]).astype(BF16)
        hidden_s[rows] = hidden
        queries = mm(hidden, wqkv_ref[0]).astype(BF16)
        keys = mm(hidden, wqkv_ref[1]).astype(BF16)
        vals = mm(hidden, wqkv_ref[2]).astype(BF16)
        down = mm_nt(cot, wout_ref[...]).astype(BF16)
        allowed = col_ref[w] == row_ref[w]
        att_parts, gq_parts, gk_parts, gv_parts = [], [], [], []
        for head in range(heads):
            cols = slice(head * HD, (head + 1) * HD)
            q, k, v, d = queries[:, cols], keys[:, cols], vals[:, cols], down[:, cols]
            table = table_ref[w, head]
            for lon_pos in range(WLON):
                start = (WLON - 1 - lon_pos) * CELL
                bias_s[head, lon_pos * CELL : (lon_pos + 1) * CELL, :] = table[
                    :, start : start + WTOK
                ]
            scores = mm_nt(q, k) * inv_scale + bias_s[head]
            scores = jnp.where(allowed, scores, -jnp.inf)
            expsum = jnp.exp(scores - jnp.max(scores, -1, keepdims=True))
            probs = expsum / jnp.sum(expsum, -1, keepdims=True)
            low = probs.astype(BF16)
            att_parts.append(mm(low, v).astype(BF16))
            dp = mm_nt(d, v)
            gv_parts.append(mm_tn(low, d).astype(BF16))
            ds = probs * (dp - jnp.sum(dp * probs, -1, keepdims=True))
            bias_s[head] = ds
            gtab_s[head] = jnp.zeros(gtab_s.shape[1:], F32)
            for lon_pos in range(WLON):
                start = (WLON - 1 - lon_pos) * CELL
                gtab_s[head, :CELL, start : start + WTOK] += bias_s[
                    head, lon_pos * CELL : (lon_pos + 1) * CELL, :
                ]
            block = pl.ds(pl.multiple_of((w * heads + head) * 16, 16), 16)
            tab_s[block] = gtab_s[head].astype(BF16)
            ds_low = ds.astype(BF16)
            gq_parts.append((mm(ds_low, k) * inv_scale).astype(BF16))
            gk_parts.append((mm_tn(ds_low, q) * inv_scale).astype(BF16))
        att = jnp.concatenate(att_parts, 1)
        att_s[rows] = att
        gq = jnp.concatenate(gq_parts, 1)
        gk = jnp.concatenate(gk_parts, 1)
        gv = jnp.concatenate(gv_parts, 1)
        grads_s[0, rows] = gq
        grads_s[1, rows] = gk
        grads_s[2, rows] = gv
        mine_s[rows, :model_width] = mm(att, wout_ref[...]).astype(BF16)
        gh = mm_nt(gq, wqkv_ref[0])
        gh = gh + mm_nt(gk, wqkv_ref[1])
        gh = (gh + mm_nt(gv, wqkv_ref[2])).astype(BF16)
        mine_s[rows, model_width:] = gh
        tp_copy(w).start()
        gain_s[group, 0:1] += jnp.sum(gh.astype(F32) * normed, 0, keepdims=True)
        return carry

    lax.fori_loop(0, windows, window, 0)

    gain_copies = [
        send(gain_s.at[group], gain_s.at[group], gain_send.at[i], gain_recv.at[i], where)
        for i, where in enumerate(group_peers)
    ]
    for copy in gain_copies:
        copy.start()

    local_width = wout_ref.shape[0]
    for member in range(3):
        wg_s[member * model_width : (member + 1) * model_width] = mm_tn(
            hidden_s[...], grads_s[member]
        ).astype(BF16)
    gout = mm_tn(att_s[...], win_s[:, model_width:]).astype(BF16)
    out_parts = model_width // local_width
    for part in range(out_parts):
        first = 3 * model_width + part * local_width
        wg_s[first : first + local_width] = gout[:, part * local_width : (part + 1) * local_width]

    half = wg_s.shape[0] // 2
    tab_half = tab_s.shape[0] // 2
    wg_mine = pl.ds(pl.multiple_of(core * half, 16), half)
    wg_other = pl.ds(pl.multiple_of((1 - core) * half, 16), half)
    tab_mine = pl.ds(pl.multiple_of(core * tab_half, 16), tab_half)
    tab_other = pl.ds(pl.multiple_of((1 - core) * tab_half, 16), tab_half)

    wg_copy = send(wg_s.at[wg_other], wg_core, core_send.at[0], core_recv.at[0], core_peer)
    wg_copy.start()

    for copy in gain_copies:
        copy.wait()
    gain_total = gain_s[0, 0:1]
    for i in range(1, n_lat * n_tp):
        gain_total = gain_total + gain_s[i, 0:1]
    tab_width = tab_s.shape[1]
    spare = jnp.concatenate(
        [gain_total, jnp.zeros((1, 2 * tab_width - model_width), F32)], 1
    )
    gtab_s[0] = tab_s[0:16].astype(F32)
    gtab_s[0, CELL : CELL + 1] = spare[:, :tab_width]
    gtab_s[0, CELL + 1 : CELL + 2] = spare[:, tab_width:]
    tab_s[0:16] = gtab_s[0].astype(BF16)
    tab_copy = send(tab_s.at[tab_other], tab_core, core_send.at[1], core_recv.at[1], core_peer)
    tab_copy.start()

    wg_copy.wait()
    wg_a[...] = (wg_s[wg_mine].astype(F32) + wg_core[...].astype(F32)).astype(BF16)
    part = half // n_lat
    lat_copies = [
        send(
            wg_a.at[pl.ds(pl.multiple_of(lax.rem(lat + d, n_lat) * part, 16), part)],
            wg_lat.at[d - 1],
            lat_send.at[d - 1],
            lat_recv.at[d - 1],
            lat_peers[d - 1],
        )
        for d in range(1, n_lat)
    ]
    for copy in lat_copies:
        copy.start()
    tab_copy.wait()
    tab_a[...] = (tab_s[tab_mine].astype(F32) + tab_core[...].astype(F32)).astype(BF16)
    tab_piece = tab_half // n_z
    tabz_copies = [
        send(
            tab_a.at[pl.ds(pl.multiple_of(lax.rem(z + d, n_z) * tab_piece, 16), tab_piece)],
            tab_z.at[d - 1],
            tz_send.at[d - 1],
            tz_recv.at[d - 1],
            z_peers[d - 1],
        )
        for d in range(1, n_z)
    ]
    for copy in tabz_copies:
        copy.start()
    for copy in lat_copies:
        copy.wait()
    total = wg_a[pl.ds(pl.multiple_of(lat * part, 16), part)].astype(F32)
    for d in range(1, n_lat):
        total = total + wg_lat[d - 1].astype(F32)
    wg_b[...] = total.astype(BF16)
    piece = part // n_z
    z_copies = [
        send(
            wg_b.at[pl.ds(pl.multiple_of(lax.rem(z + d, n_z) * piece, 16), piece)],
            wg_z.at[d - 1],
            z_send.at[d - 1],
            z_recv.at[d - 1],
            z_peers[d - 1],
        )
        for d in range(1, n_z)
    ]
    for copy in z_copies:
        copy.start()
    for copy in tabz_copies:
        copy.wait()
    tab_rows = pl.ds(pl.multiple_of(z * tab_piece, 16), tab_piece)
    total = tab_a[tab_rows].astype(F32)
    for d in range(1, n_z):
        total = total + tab_z[d - 1].astype(F32)
    tab_zg[tab_rows] = total.astype(BF16)
    tabg_copies = [
        send(
            tab_zg.at[tab_rows],
            tab_zg.at[tab_rows],
            tz_send.at[n_z - 1 + d - 1],
            tz_recv.at[n_z - 1 + d - 1],
            z_peers[d - 1],
        )
        for d in range(1, n_z)
    ]
    for copy in tabg_copies:
        copy.start()

    def arrive(w, carry):
        tp_copy(w).wait()
        return carry

    lax.fori_loop(0, windows, arrive, 0)
    win_s[...] = (mine_s[...].astype(F32) + theirs_s[...].astype(F32)).astype(BF16)
    pack_s[...] = mm(arrived_t_ref[...], win_s[...]).astype(BF16)
    back = [
        send(
            pack_s.at[pl.ds(start, size)],
            back_s.at[pl.ds(start, size)],
            out_send.at[i],
            out_recv.at[i],
            after[i],
        )
        for i, (start, size) in enumerate(starts)
    ]
    for copy in back:
        copy.start()

    for copy in z_copies:
        copy.wait()
    z_rows = pl.ds(pl.multiple_of(z * piece, 16), piece)
    total = wg_b[z_rows].astype(F32)
    for d in range(1, n_z):
        total = total + wg_z[d - 1].astype(F32)
    wg_zg[z_rows] = total.astype(BF16)
    zg_copies = [
        send(
            wg_zg.at[z_rows],
            wg_zg.at[z_rows],
            z_send.at[n_z - 1 + d - 1],
            z_recv.at[n_z - 1 + d - 1],
            z_peers[d - 1],
        )
        for d in range(1, n_z)
    ]
    for copy in zg_copies:
        copy.start()

    for copy in tabg_copies:
        copy.wait()
    tab_core_copy = send(
        tab_zg, tab_cg, core_send.at[2], core_recv.at[2], core_peer
    )
    tab_core_copy.start()

    mine_s[...] = mm(own_t_ref[...], win_s[...]).astype(BF16)
    for copy in back:
        copy.wait()
    mine_s[...] += mm(gather_t_ref[...], back_s[...]).astype(BF16)

    for copy in zg_copies:
        copy.wait()
    lat_rows = pl.ds(pl.multiple_of(lat * part, 16), part)
    wg_lg[lat_rows] = wg_zg[...]
    latg_copies = [
        send(
            wg_zg,
            wg_lg.at[lat_rows],
            lat_send.at[n_lat - 1 + d - 1],
            lat_recv.at[n_lat - 1 + d - 1],
            lat_peers[d - 1],
        )
        for d in range(1, n_lat)
    ]
    for copy in latg_copies:
        copy.start()

    def finish(w, carry):
        rows = pl.ds(pl.multiple_of(w * WTOK, 16), WTOK)
        values = x_ref[rows, :model_width].astype(F32)
        out_ref[rows] = (values + mine_s[rows, :model_width].astype(F32)).astype(BF16)
        shifted = values - jnp.mean(values, -1, keepdims=True)
        inv_std = lax.rsqrt(jnp.mean(shifted * shifted, -1, keepdims=True) + 1e-05)
        normed = shifted * inv_std
        scaled = mine_s[rows, model_width:].astype(F32) * gain_ref[...]
        glat_ref[rows] = (
            x_ref[rows, model_width:].astype(F32)
            + inv_std
            * (
                scaled
                - jnp.mean(scaled, -1, keepdims=True)
                - normed * jnp.mean(scaled * normed, -1, keepdims=True)
            )
        ).astype(BF16)
        return carry

    lax.fori_loop(0, windows, finish, 0)

    tab_core_copy.wait()
    tab_s[tab_mine] = tab_zg[...]
    tab_s[tab_other] = tab_cg[...]
    gtab_ref[...] = tab_s[...]
    last = tab_s[0:16].astype(F32)
    ggain_ref[...] = jnp.concatenate(
        [last[CELL : CELL + 1], last[CELL + 1 : CELL + 2, : model_width - tab_width]], 1
    )

    for copy in latg_copies:
        copy.wait()
    wg_core_copy = send(
        wg_lg, wg_cg, core_send.at[3], core_recv.at[3], core_peer
    )
    wg_core_copy.start()
    wg_core_copy.wait()
    wg_s[wg_mine] = wg_lg[...]
    wg_s[wg_other] = wg_cg[...]
    for member in range(3):
        gqkv_ref[member] = wg_s[member * model_width : (member + 1) * model_width].astype(F32)
    for p in range(out_parts):
        first = 3 * model_width + p * local_width
        gout_ref[:, p * local_width : (p + 1) * local_width] = wg_s[
            first : first + local_width
        ].astype(F32)


def fused(joined, ln_gain, w_qkv, w_out, table, region, layout):
    gather, own, arrived, starts = layout
    tokens, both = joined.shape
    model_width = both // 2
    local_width = w_out.shape[0]
    heads = local_width // HD
    windows = tokens // WTOK
    n_lon, n_lat, n_tp = (lax.axis_size(name) for name in ("lon", "lat", "tp"))
    n_z = n_lon // 2
    halo_rows = gather.shape[0]
    weight_rows = 3 * model_width + (model_width // local_width) * local_width
    half = weight_rows // 2
    part = half // n_lat
    piece = part // n_z
    tab_rows = windows * heads * 16
    tab_width = round_up(WIDE, 128)
    tab_half = tab_rows // 2
    cfg = (heads, windows, starts, n_lon, n_lat, n_tp)
    vmem = pl.BlockSpec(memory_space=pltpu.VMEM)
    dma = pltpu.SemaphoreType.DMA
    constants = [
        jnp.asarray(m, BF16)
        for m in (gather, own, arrived, gather.T.copy(), own.T.copy(), arrived.T.copy())
    ]
    return pl.pallas_call(
        lambda *refs: fused_kernel(cfg, *refs),
        in_specs=[vmem] * 13,
        out_specs=[vmem] * 6,
        out_shape=[
            jax.ShapeDtypeStruct((tokens, model_width), BF16),
            jax.ShapeDtypeStruct((tokens, model_width), BF16),
            jax.ShapeDtypeStruct((3, model_width, local_width), F32),
            jax.ShapeDtypeStruct((local_width, model_width), F32),
            jax.ShapeDtypeStruct((tab_rows, tab_width), BF16),
            jax.ShapeDtypeStruct((1, model_width), F32),
        ],
        scratch_shapes=[
            pltpu.VMEM((halo_rows, both), BF16),
            pltpu.VMEM((halo_rows, both), BF16),
            pltpu.VMEM((halo_rows, both), BF16),
            pltpu.VMEM((tokens, both), BF16),
            pltpu.VMEM((tokens, model_width), BF16),
            pltpu.VMEM((3, tokens, local_width), BF16),
            pltpu.VMEM((tokens, local_width), BF16),
            pltpu.VMEM((heads, WTOK, WTOK), F32),
            pltpu.VMEM((heads, 16, tab_width), F32),
            pltpu.VMEM((tokens, both), BF16),
            pltpu.VMEM((tokens, both), BF16),
            pltpu.VMEM((weight_rows, local_width), BF16),
            pltpu.VMEM((half, local_width), BF16),
            pltpu.VMEM((half, local_width), BF16),
            pltpu.VMEM((n_lat - 1, part, local_width), BF16),
            pltpu.VMEM((part, local_width), BF16),
            pltpu.VMEM((n_z - 1, piece, local_width), BF16),
            pltpu.VMEM((part, local_width), BF16),
            pltpu.VMEM((half, local_width), BF16),
            pltpu.VMEM((half, local_width), BF16),
            pltpu.VMEM((tab_rows, tab_width), BF16),
            pltpu.VMEM((tab_half, tab_width), BF16),
            pltpu.VMEM((tab_half, tab_width), BF16),
            pltpu.VMEM((n_z - 1, tab_half // n_z, tab_width), BF16),
            pltpu.VMEM((tab_half, tab_width), BF16),
            pltpu.VMEM((tab_half, tab_width), BF16),
            pltpu.VMEM((n_lat * n_tp, 8, model_width), F32),
            dma((3,)),
            dma((3,)),
            dma((windows,)),
            dma((windows,)),
            dma((3,)),
            dma((3,)),
            dma((4,)),
            dma((4,)),
            dma((2 * (n_lat - 1),)),
            dma((2 * (n_lat - 1),)),
            dma((2 * (n_z - 1),)),
            dma((2 * (n_z - 1),)),
            dma((2 * (n_z - 1),)),
            dma((2 * (n_z - 1),)),
            dma((n_lat * n_tp - 1,)),
            dma((n_lat * n_tp - 1,)),
        ],
        compiler_params=pltpu.CompilerParams(
            vmem_limit_bytes=48 * 1024 * 1024, collective_id=0, has_side_effects=True
        ),
        cost_estimate=pl.CostEstimate(
            flops=8 * 10**9, bytes_accessed=16 * 10**6, transcendentals=331776
        ),
    )(
        joined,
        ln_gain.reshape(1, -1),
        w_qkv,
        w_out,
        table,
        region[:, :, None],
        region[:, None, :],
        *constants,
    )


def on_device(latent, cotangent, ln_gain, w_qkv, w_out, bias_table):
    lon_cells, lat_cells, lev_cells, model_width = latent.shape
    head_count = w_out.shape[0] // HD
    lat_bands = lat_cells // WLAT
    lev_bands = lev_cells // WLEV
    lon_bands = lon_cells // WLON
    windows = lat_bands * lev_bands * lon_bands
    spread = spread_matrices()
    layout = halo_layout(lon_cells, lat_cells, lev_cells)
    joined = jnp.concatenate(
        [latent.reshape(-1, model_width), cotangent.reshape(-1, model_width)], 1
    )

    last_device = lax.axis_index("lat") == lax.axis_size("lat") - 1
    position = np.arange(WTOK)
    lat_edge = position % WLAT >= WLAT - WLAT // 2
    lev_edge = position // WLAT % WLEV >= WLEV - WLEV // 2
    lat_last = last_device & (jnp.arange(lat_bands) == lat_bands - 1)
    lev_last = jnp.arange(lev_bands) == lev_bands - 1
    region = (
        2.0 * (lat_last[:, None] & lat_edge).astype(F32)[:, None]
        + (lev_last[:, None] & lev_edge).astype(F32)[None]
    )
    region = jnp.broadcast_to(region[:, :, None], (lat_bands, lev_bands, lon_bands, WTOK))
    region = region.reshape(windows, WTOK)

    grouped = bias_table.reshape(
        lat_bands, lev_bands, head_count, WLEV, WLEV, WLAT, WLAT * NDIFF
    )
    table = sum(
        jnp.einsum(
            "abhtrd,dw->abhtrw", grouped[:, :, :, :, lev], spread[lev], precision=lax.Precision.HIGHEST
        )
        for lev in range(WLEV)
    )
    table = table.reshape(lat_bands * lev_bands, head_count, CELL, WIDE)
    if lon_bands > 1:
        table = jnp.repeat(table, lon_bands, axis=0)

    output, grad_latent, grad_wqkv, grad_wout, grad_tab, grad_gain = fused(
        joined, ln_gain, w_qkv, w_out, table, region, layout
    )
    grad_tab = grad_tab.reshape(lat_bands * lev_bands, lon_bands, head_count, 16, -1)
    grad_tab = grad_tab[:, :, :, :CELL, :WIDE]
    if lon_bands > 1:
        grad_tab = jnp.sum(grad_tab.astype(F32), 1).astype(BF16)
    grad_tab = grad_tab.reshape(lat_bands, lev_bands, head_count, WLEV, WLAT, WIDE)
    grad_bias = jnp.stack(
        [
            jnp.einsum(
                "abhtrw,dw->abhtrd", grad_tab, spread[lev].astype(BF16), preferred_element_type=F32
            )
            for lev in range(WLEV)
        ],
        axis=4,
    ).reshape(bias_table.shape)
    return (
        output.reshape(latent.shape),
        grad_latent.reshape(latent.shape),
        grad_gain.reshape(ln_gain.shape),
        grad_wqkv,
        grad_wout,
        grad_bias,
    )


def solution(mesh):
    return jax.shard_map(
        on_device,
        mesh=mesh,
        in_specs=(
            P("lon", "lat", None, None),
            P("lon", "lat", None, None),
            P(),
            P(None, None, "tp"),
            P("tp", None),
            P("lat", None, "tp", None),
        ),
        out_specs=(
            P("lon", "lat", None, None),
            P("lon", "lat", None, None),
            P(),
            P(None, None, "tp"),
            P("tp", None),
            P("lat", None, "tp", None),
        ),
        check_vma=False,
    )
```

```python
import math

import jax
import jax.numpy as jnp
import numpy as np
from jax import lax
from jax.experimental import pallas as pl
from jax.experimental.pallas import tpu as pltpu
from jax.sharding import PartitionSpec as P

HD = 64
WLON = 12
WLAT = 6
WLEV = 2
WTOK = 144
NREL = 3312
NDIFF = 2 * WLON - 1
CELL = WLAT * WLEV
WIDE = NDIFF * CELL
F32 = jnp.float32
BF16 = jnp.bfloat16


def spread_matrices():
    spread = np.zeros((WLEV, WLAT * NDIFF, WIDE), np.float32)
    for lev in range(WLEV):
        for row in range(WLAT):
            for diff in range(NDIFF):
                spread[lev, row * NDIFF + diff, diff * CELL + lev * WLAT + row] = 1.0
    return spread


def mm(a, b):
    return lax.dot_general(a, b, (((1,), (0,)), ((), ())), preferred_element_type=F32)


def mm_nt(a, b):
    return lax.dot_general(a, b, (((1,), (1,)), ((), ())), preferred_element_type=F32)


def mm_tn(a, b):
    return lax.dot_general(a, b, (((0,), (0,)), ((), ())), preferred_element_type=F32)


def round_up(count, to):
    return -(-count // to) * to


def halo_layout(lon_cells, lat_cells, lev_cells):
    lon_half, lat_half, lev_half = WLON // 2, WLAT // 2, WLEV // 2
    tokens = lon_cells * lat_cells * lev_cells
    cells = np.arange(tokens).reshape(lon_cells, lat_cells, lev_cells)
    pieces = [
        cells[:lon_half, lat_half:],
        cells[lon_half:, :lat_half],
        cells[:lon_half, :lat_half],
    ]
    starts, total = [], 0
    for piece in pieces:
        starts.append((total, round_up(piece.size, 16)))
        total += round_up(piece.size, 16)
    gather = np.zeros((total, tokens), np.float32)
    slots = []
    for piece, (start, _) in zip(pieces, starts):
        gather[start + np.arange(piece.size), piece.reshape(-1)] = 1.0
        slots.append(tokens + start + np.arange(piece.size).reshape(piece.shape))
    near = np.concatenate([cells[lon_half:, lat_half:], slots[1]], 1)
    far = np.concatenate([slots[0], slots[2]], 1)
    rolled = np.roll(np.concatenate([near, far], 0), -lev_half, axis=2)
    lonb, latb, levb = lon_cells // WLON, lat_cells // WLAT, lev_cells // WLEV
    order = rolled.reshape(lonb, WLON, latb, WLAT, levb, WLEV)
    order = order.transpose(2, 4, 0, 1, 5, 3).reshape(-1)
    place = np.zeros((tokens, tokens + total), np.float32)
    place[np.arange(tokens), order] = 1.0
    return gather, place[:, :tokens], place[:, tokens:], starts


class Refs:
    pass


def fused_kernel(cfg, names, *refs):
    heads, windows, starts, n_lon, n_lat, n_tp, bands = cfg
    lat_bands, lev_bands, lon_bands = bands
    r = Refs()
    for name, ref in zip(names, refs):
        setattr(r, name, ref)
    n_z = n_lon // 2
    model_width = r.gain.shape[1]
    local_width = r.wout.shape[0]
    inv_scale = 1.0 / math.sqrt(HD)
    lon, lat, tp = lax.axis_index("lon"), lax.axis_index("lat"), lax.axis_index("tp")
    z, core = lax.div(lon, 2), lax.rem(lon, 2)
    sibling = lon + 1 - 2 * core
    group = lat * n_tp + tp

    def device(lon_at, lat_at, tp_at):
        return {"lon": lon_at, "lat": lat_at, "tp": tp_at}

    def send(src, dst, sems, index, where):
        return pltpu.make_async_remote_copy(
            src_ref=src,
            dst_ref=dst,
            send_sem=sems.at[0, index],
            recv_sem=sems.at[1, index],
            device_id=where,
            device_id_type=pl.DeviceIdType.MESH,
        )

    def aligned(start, size):
        return pl.ds(pl.multiple_of(start, 16), size)

    lon_next, lon_prev = lax.rem(lon + 1, n_lon), lax.rem(lon + n_lon - 1, n_lon)
    lat_next, lat_prev = lax.rem(lat + 1, n_lat), lax.rem(lat + n_lat - 1, n_lat)
    before = [
        device(lon_prev, lat, tp),
        device(lon, lat_prev, tp),
        device(lon_prev, lat_prev, tp),
    ]
    after = [
        device(lon_next, lat, tp),
        device(lon, lat_next, tp),
        device(lon_next, lat_next, tp),
    ]
    z_peers = [device(lax.rem(z + d, n_z) * 2 + core, lat, tp) for d in range(1, n_z)]
    lat_peers = [device(lon, lax.rem(lat + d, n_lat), tp) for d in range(1, n_lat)]
    group_peers = []
    for d in range(1, n_lat * n_tp):
        other = lax.rem(group + d, n_lat * n_tp)
        group_peers.append(device(lon, lax.div(other, n_tp), lax.rem(other, n_tp)))
    core_peer = device(sibling, lat, tp)
    tp_peer = device(lon, lat, lax.rem(tp + 1, n_tp))

    barrier = pltpu.get_barrier_semaphore()
    greeted = before + after + z_peers + group_peers + [core_peer]
    for where in greeted:
        pl.semaphore_signal(
            barrier, inc=1, device_id=where, device_id_type=pl.DeviceIdType.MESH
        )
    loads = [
        pltpu.make_async_copy(getattr(r, name + "_hbm"), getattr(r, name), r.load_sem.at[i])
        for i, name in enumerate(MATRICES)
    ]
    for copy in loads:
        copy.start()
    loads[0].wait()
    r.pack[...] = mm(r.gather[...], r.x[...]).astype(BF16)
    pl.semaphore_wait(barrier, len(greeted))
    halo = [
        send(r.pack.at[pl.ds(a, n)], r.halo.at[pl.ds(a, n)], r.in_sem, i, before[i])
        for i, (a, n) in enumerate(starts)
    ]
    for copy in halo:
        copy.start()
    wout_copy = send(r.wout, r.wout_their, r.wo_sem, 0, tp_peer)
    wout_copy.start()
    for copy in loads[1:]:
        copy.wait()
    r.win[...] = mm(r.own[...], r.x[...]).astype(BF16)

    types = lat_bands * lev_bands
    run = WLAT * NDIFF
    for kind in range(types):
        block = r.bias_in.at[kind // lev_bands, kind % lev_bands]
        for lev_t in range(WLEV):
            for lev_u in range(WLEV):
                for row in range(WLAT):
                    first = ((lev_t * WLEV + lev_u) * WLAT + row) * run
                    rows = block[:, first : first + run]
                    for head in range(heads):
                        r.table_in[
                            lev_u, kind * heads + head, lev_t * WLAT + row : lev_t * WLAT + row + 1, :
                        ] = rows[head : head + 1]
    total = None
    for lev_u in range(WLEV):
        rest = r.table_in[lev_u].reshape(types * heads * 16, run)
        for _ in range(3):
            piece = rest.astype(BF16)
            rest = rest - piece.astype(F32)
            term = mm(piece, r.spread[lev_u])
            total = term if total is None else total + term
    r.table[...] = total.reshape(types * heads, 16, WIDE)

    for copy in halo:
        copy.wait()
    r.win[...] += mm(r.arrived[...], r.halo[...]).astype(BF16)

    def att_copy(w):
        rows = aligned(w * WTOK, WTOK)
        return send(r.att.at[rows], r.att_their.at[rows], r.att_sem, w, tp_peer)

    def gh_copy(w):
        rows = aligned(w * WTOK, WTOK)
        return send(r.gh.at[rows], r.gh_their.at[rows], r.gh_sem, w, tp_peer)

    def forward(w, carry):
        rows = aligned(w * WTOK, WTOK)
        x = r.win[rows, :model_width].astype(F32)
        cot = r.win[rows, model_width:]
        shifted = x - jnp.mean(x, -1, keepdims=True)
        inv_std = lax.rsqrt(jnp.mean(shifted * shifted, -1, keepdims=True) + 1e-05)
        normed = shifted * inv_std
        r.normed[rows] = normed
        hidden = (normed * r.gain[...]).astype(BF16)
        r.hidden[rows] = hidden
        queries = mm(hidden, r.wqkv[0]).astype(BF16)
        keys = mm(hidden, r.wqkv[1]).astype(BF16)
        vals = mm(hidden, r.wqkv[2]).astype(BF16)
        down = mm_nt(cot, r.wout[...]).astype(BF16)
        r.query[rows] = queries
        r.key[rows] = keys
        kind = lax.div(w, lon_bands)
        last_lat = (lat == n_lat - 1) & (lax.div(kind, lev_bands) == lat_bands - 1)
        last_lev = lax.rem(kind, lev_bands) == lev_bands - 1
        lat_flag = jnp.where(last_lat, 2.0, 0.0)
        lev_flag = jnp.where(last_lev, 1.0, 0.0)
        col = r.col[:, 0:1] * lat_flag + r.col[:, 1:2] * lev_flag
        row = r.row[0:1] * lat_flag + r.row[1:2] * lev_flag
        allowed = col == row
        att_parts, gv_parts = [], []
        for head in range(heads):
            cols = slice(head * HD, (head + 1) * HD)
            q, k, v, d = queries[:, cols], keys[:, cols], vals[:, cols], down[:, cols]
            table = r.table[kind * heads + head]
            for lon_pos in range(WLON):
                start = (WLON - 1 - lon_pos) * CELL
                r.ds[w * heads + head, lon_pos * CELL : (lon_pos + 1) * CELL, :] = table[
                    :CELL, start : start + WTOK
                ]
            scores = mm_nt(q, k) * inv_scale + r.ds[w * heads + head]
            scores = jnp.where(allowed, scores, -jnp.inf)
            expsum = jnp.exp(scores - jnp.max(scores, -1, keepdims=True))
            probs = expsum / jnp.sum(expsum, -1, keepdims=True)
            low = probs.astype(BF16)
            att_parts.append(mm(low, v).astype(BF16))
            dp = mm_nt(d, v)
            gv_parts.append(mm_tn(low, d).astype(BF16))
            r.ds[w * heads + head] = probs * (dp - jnp.sum(dp * probs, -1, keepdims=True))
        r.att[rows] = jnp.concatenate(att_parts, 1)
        att_copy(w).start()
        r.grads[2, rows] = jnp.concatenate(gv_parts, 1)
        return carry

    lax.fori_loop(0, windows, forward, 0)

    blocks = local_width // 128

    class Chunk:
        def __init__(self, index):
            self.base = index * 4
            self.index = index
            rows = r.wg.shape[1]
            self.half, self.part = rows // 2, rows // 2 // n_lat
            self.piece = self.part // n_z
            self.full = r.wg.at[index]
            self.mine = aligned(core * self.half, self.half)
            self.other = aligned((1 - core) * self.half, self.half)
            self.lat_rows = aligned(lat * self.part, self.part)
            self.z_rows = aligned(z * self.piece, self.piece)
            i = index
            self.core_a = send(self.full.at[self.other], r.wg_core.at[i], r.core_sem, 2 * i, core_peer)
            self.core_b = send(r.wg_lg.at[i], r.wg_cg.at[i], r.core_sem, 2 * i + 1, core_peer)
            lat_base, z_base = i * 2 * (n_lat - 1), i * 2 * (n_z - 1)
            self.lat_a, self.lat_b, self.z_a, self.z_b = [], [], [], []
            for d in range(1, n_lat):
                rows_d = aligned(lax.rem(lat + d, n_lat) * self.part, self.part)
                self.lat_a.append(
                    send(r.wg_a.at[i, rows_d], r.wg_lat.at[i, d - 1], r.lat_sem, lat_base + d - 1, lat_peers[d - 1])
                )
                self.lat_b.append(
                    send(
                        r.wg_zg.at[i],
                        r.wg_lg.at[i, self.lat_rows],
                        r.lat_sem,
                        lat_base + n_lat - 1 + d - 1,
                        lat_peers[d - 1],
                    )
                )
            for d in range(1, n_z):
                rows_d = aligned(lax.rem(z + d, n_z) * self.piece, self.piece)
                self.z_a.append(
                    send(r.wg_b.at[i, rows_d], r.wg_z.at[i, d - 1], r.z_sem, z_base + d - 1, z_peers[d - 1])
                )
                self.z_b.append(
                    send(
                        r.wg_zg.at[i, self.z_rows],
                        r.wg_zg.at[i, self.z_rows],
                        r.z_sem,
                        z_base + n_z - 1 + d - 1,
                        z_peers[d - 1],
                    )
                )

        def to_core(self):
            self.core_a.start()

        def to_lat(self):
            self.core_a.wait()
            i = self.index
            r.wg_a[i] = (self.full[self.mine].astype(F32) + r.wg_core[i].astype(F32)).astype(BF16)
            for copy in self.lat_a:
                copy.start()

        def to_z(self):
            for copy in self.lat_a:
                copy.wait()
            i = self.index
            total = r.wg_a[i, self.lat_rows].astype(F32)
            for d in range(1, n_lat):
                total = total + r.wg_lat[i, d - 1].astype(F32)
            r.wg_b[i] = total.astype(BF16)
            for copy in self.z_a:
                copy.start()

        def from_z(self):
            for copy in self.z_a:
                copy.wait()
            i = self.index
            total = r.wg_b[i, self.z_rows].astype(F32)
            for d in range(1, n_z):
                total = total + r.wg_z[i, d - 1].astype(F32)
            r.wg_zg[i, self.z_rows] = total.astype(BF16)
            for copy in self.z_b:
                copy.start()

        def from_lat(self):
            for copy in self.z_b:
                copy.wait()
            r.wg_lg[self.index, self.lat_rows] = r.wg_zg[self.index]
            for copy in self.lat_b:
                copy.start()

        def from_core(self):
            for copy in self.lat_b:
                copy.wait()
            self.core_b.start()

        def end(self):
            self.core_b.wait()
            self.full[self.mine] = r.wg_lg[self.index]
            self.full[self.other] = r.wg_cg[self.index]

    def put(chunk, first, grad):
        size = grad.shape[0]
        for b in range(grad.shape[1] // 128):
            r.wg[chunk, first + b * size : first + (b + 1) * size] = grad[
                :, b * 128 : (b + 1) * 128
            ].astype(BF16)

    def take(chunk, first, ref, size, columns):
        for b in range(columns // 128):
            ref[:, b * 128 : (b + 1) * 128] = r.wg[
                chunk, first + b * size : first + (b + 1) * size
            ].astype(F32)

    one, two = Chunk(0), Chunk(1)
    second = blocks * model_width
    put(0, 0, mm_tn(r.hidden[...], r.grads[2]))
    put(0, second, mm_tn(r.att[...], r.win[:, model_width:]))
    one.to_core()

    r.gain_part[group] = jnp.zeros(r.gain_part.shape[1:], F32)

    def backward(w, carry):
        rows = aligned(w * WTOK, WTOK)
        gq_parts, gk_parts = [], []
        for head in range(heads):
            cols = slice(head * HD, (head + 1) * HD)
            r.gtab[head] = jnp.zeros(r.gtab.shape[1:], F32)
            for lon_pos in range(WLON):
                start = (WLON - 1 - lon_pos) * CELL
                r.gtab[head, :CELL, start : start + WTOK] += r.ds[
                    w * heads + head, lon_pos * CELL : (lon_pos + 1) * CELL, :
                ]
            r.tab[aligned((w * heads + head) * 16, 16)] = r.gtab[head].astype(BF16)
            ds_low = r.ds[w * heads + head].astype(BF16)
            q, k = r.query[rows, cols], r.key[rows, cols]
            gq_parts.append((mm(ds_low, k) * inv_scale).astype(BF16))
            gk_parts.append((mm_tn(ds_low, q) * inv_scale).astype(BF16))
        gq = jnp.concatenate(gq_parts, 1)
        gk = jnp.concatenate(gk_parts, 1)
        r.grads[0, rows] = gq
        r.grads[1, rows] = gk
        gh = mm_nt(gq, r.wqkv[0])
        gh = gh + mm_nt(gk, r.wqkv[1])
        gh = (gh + mm_nt(r.grads[2, rows], r.wqkv[2])).astype(BF16)
        r.gh[rows] = gh
        gh_copy(w).start()
        r.gain_part[group, 0:1] += jnp.sum(gh.astype(F32) * r.normed[rows], 0, keepdims=True)
        return carry

    middle = windows // 2
    lax.fori_loop(0, middle, backward, 0)
    one.to_lat()
    lax.fori_loop(middle, windows, backward, 0)

    gain_copies = [
        send(r.gain_part.at[group], r.gain_part.at[group], r.gain_sem, i, where)
        for i, where in enumerate(group_peers)
    ]
    for copy in gain_copies:
        copy.start()
    put(1, 0, mm_tn(r.hidden[...], r.grads[0]))
    put(1, second, mm_tn(r.hidden[...], r.grads[1]))
    two.to_core()
    one.to_z()

    def arrive_att(w, carry):
        att_copy(w).wait()
        return carry

    wout_copy.wait()
    lax.fori_loop(0, windows, arrive_att, 0)
    mine = mm(r.att[...], r.wout[...]).astype(BF16)
    theirs = mm(r.att_their[...], r.wout_their[...]).astype(BF16)
    r.sums[:, :model_width] = (mine.astype(F32) + theirs.astype(F32)).astype(BF16)
    two.to_lat()

    def leave(index, columns):
        r.back[index] = mm(r.arrived_t[...], r.sums[:, columns]).astype(BF16)
        copies = [
            send(
                r.back.at[index, pl.ds(a, n)],
                r.came.at[index, pl.ds(a, n)],
                r.out_sem,
                3 * index + i,
                after[i],
            )
            for i, (a, n) in enumerate(starts)
        ]
        for copy in copies:
            copy.start()
        return copies

    out_copies = leave(0, slice(0, model_width))

    for copy in gain_copies:
        copy.wait()
    gain_total = r.gain_part[0, 0:1]
    for i in range(1, n_lat * n_tp):
        gain_total = gain_total + r.gain_part[i, 0:1]
    tab_width = r.tab.shape[1]
    spare = jnp.concatenate([gain_total, jnp.zeros((1, 2 * tab_width - model_width), F32)], 1)
    r.gtab[0] = r.tab[0:16].astype(F32)
    r.gtab[0, CELL : CELL + 1] = spare[:, :tab_width]
    r.gtab[0, CELL + 1 : CELL + 2] = spare[:, tab_width:]
    r.tab[0:16] = r.gtab[0].astype(BF16)
    tab_half = r.tab.shape[0] // 2
    tab_piece = tab_half // n_z
    tab_mine = aligned(core * tab_half, tab_half)
    tab_other = aligned((1 - core) * tab_half, tab_half)
    tab_rows = aligned(z * tab_piece, tab_piece)
    tab_a = send(r.tab.at[tab_other], r.tab_core, r.core_sem, 4, core_peer)
    tab_a.start()

    one.from_z()
    two.to_z()
    tab_a.wait()
    r.tab_a[...] = (r.tab[tab_mine].astype(F32) + r.tab_core[...].astype(F32)).astype(BF16)
    tabz = [
        send(
            r.tab_a.at[aligned(lax.rem(z + d, n_z) * tab_piece, tab_piece)],
            r.tab_z.at[d - 1],
            r.tz_sem,
            d - 1,
            z_peers[d - 1],
        )
        for d in range(1, n_z)
    ]
    for copy in tabz:
        copy.start()

    def arrive_gh(w, carry):
        gh_copy(w).wait()
        return carry

    lax.fori_loop(0, windows, arrive_gh, 0)
    r.sums[:, model_width:] = (r.gh[...].astype(F32) + r.gh_their[...].astype(F32)).astype(BF16)
    gh_copies = leave(1, slice(model_width, 2 * model_width))
    r.back_own[...] = mm(r.own_t[...], r.sums[...]).astype(BF16)

    one.from_lat()
    for copy in tabz:
        copy.wait()
    total = r.tab_a[tab_rows].astype(F32)
    for d in range(1, n_z):
        total = total + r.tab_z[d - 1].astype(F32)
    r.tab_zg[tab_rows] = total.astype(BF16)
    tabg = [
        send(
            r.tab_zg.at[tab_rows],
            r.tab_zg.at[tab_rows],
            r.tz_sem,
            n_z - 1 + d - 1,
            z_peers[d - 1],
        )
        for d in range(1, n_z)
    ]
    for copy in tabg:
        copy.start()
    two.from_z()

    for copy in out_copies:
        copy.wait()
    out_own = r.back_own[:, :model_width] + mm(r.gather_t[...], r.came[0]).astype(BF16)
    r.out[...] = (r.x[:, :model_width].astype(F32) + out_own.astype(F32)).astype(BF16)

    one.from_core()
    for copy in tabg:
        copy.wait()
    tab_b = send(r.tab_zg, r.tab_cg, r.core_sem, 5, core_peer)
    tab_b.start()

    for copy in gh_copies:
        copy.wait()
    r.gh_own[...] = r.back_own[:, model_width:] + mm(r.gather_t[...], r.came[1]).astype(BF16)
    two.from_lat()

    def finish(w, carry):
        rows = aligned(w * WTOK, WTOK)
        values = r.x[rows, :model_width].astype(F32)
        shifted = values - jnp.mean(values, -1, keepdims=True)
        inv_std = lax.rsqrt(jnp.mean(shifted * shifted, -1, keepdims=True) + 1e-05)
        normed = shifted * inv_std
        scaled = r.gh_own[rows].astype(F32) * r.gain[...]
        r.glat[rows] = (
            r.x[rows, model_width:].astype(F32)
            + inv_std
            * (
                scaled
                - jnp.mean(scaled, -1, keepdims=True)
                - normed * jnp.mean(scaled * normed, -1, keepdims=True)
            )
        ).astype(BF16)
        return carry

    lax.fori_loop(0, windows, finish, 0)

    one.end()
    take(0, 0, r.gqkv.at[2], model_width, local_width)
    take(0, second, r.gout, local_width, model_width)

    tab_b.wait()
    r.tab[tab_mine] = r.tab_zg[...]
    r.tab[tab_other] = r.tab_cg[...]
    last = r.tab[0:16].astype(F32)
    r.ggain[...] = jnp.concatenate(
        [last[CELL : CELL + 1], last[CELL + 1 : CELL + 2, : model_width - tab_width]], 1
    )
    for lev_u in range(WLEV):
        r.table_out[lev_u] = mm_nt(r.tab[:, :WIDE], r.spread[lev_u]).reshape(
            windows * heads, 16, run
        )
    for kind in range(types):
        block = r.gbias.at[kind // lev_bands, kind % lev_bands]
        for lev_t in range(WLEV):
            for lev_u in range(WLEV):
                for row in range(WLAT):
                    first = ((lev_t * WLEV + lev_u) * WLAT + row) * run
                    cell = lev_t * WLAT + row
                    for head in range(heads):
                        total = None
                        for c in range(lon_bands):
                            at = (kind * lon_bands + c) * heads + head
                            term = r.table_out[lev_u, at, cell : cell + 1, :]
                            total = term if total is None else total + term
                        block[head : head + 1, first : first + run] = total

    two.from_core()
    two.end()
    take(1, 0, r.gqkv.at[0], model_width, local_width)
    take(1, second, r.gqkv.at[1], model_width, local_width)


MATRICES = ("gather", "own", "arrived", "gather_t", "own_t", "arrived_t", "spread")


def fused(joined, ln_gain, w_qkv, w_out, bias_table, layout, bands):
    gather, own, arrived, starts = layout
    tokens, both = joined.shape
    width = both // 2
    local = w_out.shape[0]
    heads = local // HD
    windows = tokens // WTOK
    n_lon, n_lat, n_tp = (lax.axis_size(name) for name in ("lon", "lat", "tp"))
    n_z = n_lon // 2
    types = bands[0] * bands[1]
    run = WLAT * NDIFF
    halo_rows = gather.shape[0]
    chunk = 2 * (local // 128) * width
    half = chunk // 2
    part = half // n_lat
    piece = part // n_z
    tab_rows = windows * heads * 16
    tab_width = round_up(WIDE, 128)
    tab_half = tab_rows // 2
    cfg = (heads, windows, starts, n_lon, n_lat, n_tp, bands)
    position = np.arange(WTOK)
    edges = np.stack(
        [
            position % WLAT >= WLAT - WLAT // 2,
            position // WLAT % WLEV >= WLEV - WLEV // 2,
        ]
    ).astype(np.float32)
    matrices = {
        "gather": gather,
        "own": own,
        "arrived": arrived,
        "gather_t": gather.T.copy(),
        "own_t": own.T.copy(),
        "arrived_t": arrived.T.copy(),
        "spread": spread_matrices(),
    }
    vmem = pl.BlockSpec(memory_space=pltpu.VMEM)
    anywhere = pl.BlockSpec(memory_space=pl.ANY)

    def sems(count):
        return pltpu.SemaphoreType.DMA((2, count))

    operands = {
        "x": joined,
        "gain": ln_gain.reshape(1, -1),
        "wqkv": w_qkv,
        "wout": w_out,
        "bias_in": bias_table,
        "col": jnp.asarray(edges.T.copy()),
        "row": jnp.asarray(edges),
    }
    for name in MATRICES:
        operands[name + "_hbm"] = jnp.asarray(matrices[name], BF16)
    results = {
        "out": ((tokens, width), BF16),
        "glat": ((tokens, width), BF16),
        "ggain": ((1, width), F32),
        "gqkv": ((3, width, local), F32),
        "gout": ((local, width), F32),
        "gbias": (bias_table.shape, F32),
    }
    scratch = {name: pltpu.VMEM(matrices[name].shape, BF16) for name in MATRICES}
    for name, shape, dtype in (
        ("pack", (halo_rows, both), BF16),
        ("halo", (halo_rows, both), BF16),
        ("back", (2, halo_rows, width), BF16),
        ("came", (2, halo_rows, width), BF16),
        ("win", (tokens, both), BF16),
        ("sums", (tokens, both), BF16),
        ("back_own", (tokens, both), BF16),
        ("gh_own", (tokens, width), BF16),
        ("normed", (tokens, width), F32),
        ("hidden", (tokens, width), BF16),
        ("query", (tokens, local), BF16),
        ("key", (tokens, local), BF16),
        ("grads", (3, tokens, local), BF16),
        ("att", (tokens, local), BF16),
        ("att_their", (tokens, local), BF16),
        ("wout_their", (local, width), BF16),
        ("gh", (tokens, width), BF16),
        ("gh_their", (tokens, width), BF16),
        ("ds", (windows * heads, WTOK, WTOK), F32),
        ("gtab", (heads, 16, tab_width), F32),
        ("table_in", (WLEV, types * heads, 16, run), F32),
        ("table", (types * heads, 16, WIDE), F32),
        ("table_out", (WLEV, windows * heads, 16, run), F32),
        ("wg", (2, chunk, 128), BF16),
        ("wg_core", (2, half, 128), BF16),
        ("wg_a", (2, half, 128), BF16),
        ("wg_lat", (2, n_lat - 1, part, 128), BF16),
        ("wg_b", (2, part, 128), BF16),
        ("wg_z", (2, n_z - 1, piece, 128), BF16),
        ("wg_zg", (2, part, 128), BF16),
        ("wg_lg", (2, half, 128), BF16),
        ("wg_cg", (2, half, 128), BF16),
        ("tab", (tab_rows, tab_width), BF16),
        ("tab_core", (tab_half, tab_width), BF16),
        ("tab_a", (tab_half, tab_width), BF16),
        ("tab_z", (n_z - 1, tab_half // n_z, tab_width), BF16),
        ("tab_zg", (tab_half, tab_width), BF16),
        ("tab_cg", (tab_half, tab_width), BF16),
        ("gain_part", (n_lat * n_tp, 8, width), F32),
    ):
        scratch[name] = pltpu.VMEM(shape, dtype)
    for name, count in (
        ("in_sem", 3),
        ("wo_sem", 1),
        ("att_sem", windows),
        ("gh_sem", windows),
        ("out_sem", 6),
        ("core_sem", 6),
        ("lat_sem", 4 * (n_lat - 1)),
        ("z_sem", 4 * (n_z - 1)),
        ("tz_sem", 2 * (n_z - 1)),
        ("gain_sem", n_lat * n_tp - 1),
    ):
        scratch[name] = sems(count)
    scratch["load_sem"] = pltpu.SemaphoreType.DMA((len(MATRICES),))
    names = list(operands) + list(results) + list(scratch)
    return pl.pallas_call(
        lambda *refs: fused_kernel(cfg, names, *refs),
        in_specs=[anywhere if name.endswith("_hbm") else vmem for name in operands],
        out_specs=[vmem] * len(results),
        out_shape=[jax.ShapeDtypeStruct(*spec) for spec in results.values()],
        scratch_shapes=list(scratch.values()),
        compiler_params=pltpu.CompilerParams(
            vmem_limit_bytes=56 * 1024 * 1024, collective_id=0, has_side_effects=True
        ),
        cost_estimate=pl.CostEstimate(
            flops=8 * 10**9, bytes_accessed=16 * 10**6, transcendentals=331776
        ),
    )(*operands.values())


def on_device(latent, cotangent, ln_gain, w_qkv, w_out, bias_table):
    lon_cells, lat_cells, lev_cells, model_width = latent.shape
    bands = (lat_cells // WLAT, lev_cells // WLEV, lon_cells // WLON)
    layout = halo_layout(lon_cells, lat_cells, lev_cells)
    joined = jnp.concatenate(
        [latent.reshape(-1, model_width), cotangent.reshape(-1, model_width)], 1
    )
    output, grad_latent, grad_gain, grad_wqkv, grad_wout, grad_bias = fused(
        joined, ln_gain, w_qkv, w_out, bias_table, layout, bands
    )
    return (
        output.reshape(latent.shape),
        grad_latent.reshape(latent.shape),
        grad_gain.reshape(ln_gain.shape),
        grad_wqkv,
        grad_wout,
        grad_bias,
    )


def solution(mesh):
    return jax.shard_map(
        on_device,
        mesh=mesh,
        in_specs=(
            P("lon", "lat", None, None),
            P("lon", "lat", None, None),
            P(),
            P(None, None, "tp"),
            P("tp", None),
            P("lat", None, "tp", None),
        ),
        out_specs=(
            P("lon", "lat", None, None),
            P("lon", "lat", None, None),
            P(),
            P(None, None, "tp"),
            P("tp", None),
            P("lat", None, "tp", None),
        ),
        check_vma=False,
    )
```
